32 devices in a mesh: ha: 8 (over y, x, core), wa: 4 (over z).
Axes of the slice: x: 2, y: 2, z: 4, core: 2. Of those that a mesh axis runs over, the one named last changes fastest.
Arguments:
- token_queries: bfloat16 [16, 4, 32, 16, 128], P(None, None, 'ha', 'wa'), may hold values from -48 to 48
- token_keys: bfloat16 [16, 4, 32, 16, 128], P(None, None, 'ha', 'wa'), may hold values from -6 to 6
- token_values: bfloat16 [16, 4, 32, 16, 128], P(None, None, 'ha', 'wa'), may hold values from -6 to 6
Outputs:
- attended: bfloat16 [16, 4, 32, 16, 128], P(None, None, 'ha', 'wa')
The draws below stay inside these ranges and needn't reach their ends.
All inputs are finite; a program needn't handle non-finite values.
Results may differ from the reference program's by a relative error of at most 0.0055.
Values may be sent and summed in bfloat16 or wider, within the bound.
A program may use at most 64 MiB of HBM per device.

```python
import jax
import jax.numpy as jnp
from jax import lax

DH = 128
H = 16
LF = 4
LH = 32
LW = 16


def pair_draw(key):
    total = LF * LH * LW
    query_key = jax.random.fold_in(key, 11)
    keys_key = jax.random.fold_in(key, 12)
    queries = jnp.clip(3.0 * jax.random.normal(query_key, (H, total, DH), jnp.float32), -18.0, 18.0)
    key_rows = jnp.clip(jax.random.normal(keys_key, (H, total, DH), jnp.float32), -6.0, 6.0)
    return (queries.reshape(H, LF, LH, LW, DH), key_rows.reshape(H, LF, LH, LW, DH))


def draw_token_queries(key, part):
    return pair_draw(key)[0].astype(jnp.bfloat16)


def draw_token_keys(key, part):
    return pair_draw(key)[1].astype(jnp.bfloat16)


def block_scale(key, dims, cuts, low, largest):
    def one(position, parts):
        draws = jax.random.uniform(jax.random.fold_in(jax.random.fold_in(key, 6), position), (parts,), jnp.float32, low / len(cuts), largest / len(cuts))
        return jnp.repeat(jnp.exp(draws), dims[position] // parts).reshape((-1,) + (1,) * (len(dims) - position - 1))

    gain = one(*cuts[0])
    for cut in cuts[1:]:
        gain = gain * one(*cut)
    return gain


def noise(stream_key, shape, spread, bound, shards=(), kind=jnp.bfloat16):
    drawn = jax.random.normal(stream_key, shape, jnp.float32) * spread
    if len(shards) > 0:
        drawn = block_scale(stream_key, shape, shards, -0.22, 0.18) * drawn
    return jnp.clip(drawn, min=-bound, max=bound).astype(kind)


def setup_inputs(seed: int = 0) -> dict:
    key_of = jax.random.split(jax.random.key(seed), 4)
    return {
        "token_queries": draw_token_queries(jax.random.fold_in(key_of[3], 71), 0),
        "token_keys": draw_token_keys(jax.random.fold_in(key_of[3], 71), 0),
        "token_values": noise(key_of[2], (H, LF, LH, LW, DH), 1.0, 6.0, ((2, 8), (3, 4))),
    }


def reference(token_queries, token_keys, token_values):
    heads = token_queries.shape[0]
    head_size = token_queries.shape[-1]
    factor = head_size ** -0.5
    queries = token_queries.reshape(heads, -1, head_size)
    key_rows = token_keys.reshape(heads, -1, head_size)
    value_rows = token_values.reshape(heads, -1, head_size)
    total = queries.shape[1]
    block_size = min(1024, total)

    def one_head(triple):
        head_queries, head_keys, head_values = triple

        def attend_block(query_block):
            scores = jnp.dot(query_block, head_keys.T, preferred_element_type=jnp.float32) * factor
            weights = jnp.exp(scores - jnp.max(scores, axis=1, keepdims=True))
            totals = jnp.sum(weights, axis=1, keepdims=True)
            mixed = jnp.dot(weights.astype(jnp.bfloat16), head_values, preferred_element_type=jnp.float32)
            return (mixed / totals).astype(jnp.bfloat16)

        return lax.map(attend_block, head_queries.reshape(total // block_size, block_size, head_size))

    attended = lax.map(one_head, (queries, key_rows, value_rows))
    return attended.reshape(token_queries.shape)
```

```python
import functools

import jax
import jax.numpy as jnp
from jax import lax
from jax.experimental import pallas as pl
from jax.experimental.pallas import tpu as pltpu
from jax.sharding import PartitionSpec as P

MESH = pl.DeviceIdType.MESH
LOG2E = 1.4426950408889634
KEY_TILE = 2048
SLOTS_AT_ONCE = 4


def slot_order(subgroups, width):
    def rank(offset):
        up, across = offset
        distance = min(across, width - across)
        return (-distance, up == 0, across, up)

    return sorted(((u, w) for u in range(subgroups) for w in range(width)), key=rank)


def attend(queries, keys, values, key_count, factor):
    tile = min(KEY_TILE, key_count)
    scale = factor * LOG2E

    def scores_of(index):
        return lax.dot_general(
            queries, keys(index, tile), (((1,), (1,)), ((), ())), preferred_element_type=jnp.float32
        )

    def mix(weights, index):
        return jnp.dot(
            weights.astype(jnp.bfloat16), values(index, tile), preferred_element_type=jnp.float32
        )

    scores = scores_of(0)
    top = jnp.max(scores, axis=1, keepdims=True)
    weights = jnp.exp2((scores - top) * scale)
    total = jnp.sum(weights, axis=1, keepdims=True)
    mixed = mix(weights, 0)

    def fold(index, state):
        top, total, mixed = state
        scores = scores_of(index)
        new_top = jnp.maximum(top, jnp.max(scores, axis=1, keepdims=True))
        shrink = jnp.exp2((top - new_top) * scale)
        weights = jnp.exp2((scores - new_top) * scale)
        total = total * shrink + jnp.sum(weights, axis=1, keepdims=True)
        return new_top, total, mixed * shrink + mix(weights, index)

    if key_count > tile:
        top, total, mixed = lax.fori_loop(1, key_count // tile, fold, (top, total, mixed))
    return (mixed / total).astype(jnp.bfloat16)


def kernel(
    height, width, group, q_ref, k_ref, v_ref, o_ref, qb, kb, vb, ob,
    send_sem, recv_sem, pass_send, pass_recv,
):
    subgroups = height // group
    order = slot_order(subgroups, width)
    slots = len(order)
    own = slots - 1
    length, size = k_ref.shape[1], k_ref.shape[2]
    factor = size ** (-0.5)
    ha, wa = lax.axis_index("ha"), lax.axis_index("wa")
    member, sub = lax.rem(ha, group), lax.div(ha, group)

    def peer(slot, sign):
        up, across = order[slot]
        to_sub = lax.rem(sub + (up if sign > 0 else subgroups - up), subgroups)
        to_wa = lax.rem(wa + (across if sign > 0 else width - across), width)
        return (to_sub * group + member, to_wa), to_sub * width + to_wa

    def sibling(step):
        return (sub * group + lax.rem(member + step, group), wa)

    def each_sibling(act):
        if group == 2:
            act(1)
        elif group > 2:
            pl.loop(1, group)(act)

    my_head = sub * width + wa

    barrier = pltpu.get_barrier_semaphore()
    for slot in range(own):
        pl.semaphore_signal(barrier, inc=1, device_id=peer(slot, 1)[0], device_id_type=MESH)
    each_sibling(
        lambda step: pl.semaphore_signal(
            barrier, inc=1, device_id=sibling(step), device_id_type=MESH
        )
    )
    own_copies = [
        pltpu.make_async_copy(src.at[my_head], dst, recv_sem.at[t, own])
        for t, (src, dst) in enumerate(
            ((k_ref, kb.at[0, own]), (v_ref, vb.at[0, own]), (q_ref, qb.at[own]))
        )
    ]
    for copy in own_copies:
        copy.start()
    pl.semaphore_wait(barrier, own + group - 1)

    def to_peer(t, slot):
        src, dst = ((k_ref, kb.at[0, slot]), (v_ref, vb.at[0, slot]), (q_ref, qb.at[slot]))[t]
        device, head = peer(slot, 1)
        return pltpu.make_async_remote_copy(
            src_ref=src.at[head],
            dst_ref=dst,
            send_sem=send_sem.at[t, slot],
            recv_sem=recv_sem.at[t, slot],
            device_id=device,
            device_id_type=MESH,
        )

    sent = [[to_peer(t, slot) for slot in range(own)] for t in range(3)]
    for row in sent:
        for copy in row:
            copy.start()

    def to_sibling(t, slot, step):
        buf = (kb, vb)[t]
        return pltpu.make_async_remote_copy(
            src_ref=buf.at[0, slot],
            dst_ref=buf.at[step, slot],
            send_sem=pass_send.at[t, step - 1],
            recv_sem=pass_recv.at[t, step - 1],
            device_id=sibling(step),
            device_id_type=MESH,
        )

    for t in range(2):
        for slot in (own, *range(own)):
            if slot == own:
                own_copies[t].wait()
            else:
                sent[t][slot].wait_recv()
            each_sibling(lambda step: to_sibling(t, slot, step).start())

    def whole_pass(t, step):
        buf = (kb, vb)[t]
        return pltpu.make_async_remote_copy(
            src_ref=buf.at[0],
            dst_ref=buf.at[step],
            send_sem=pass_send.at[t, step - 1],
            recv_sem=pass_recv.at[t, step - 1],
            device_id=sibling(step),
            device_id_type=MESH,
        )

    for t in range(2):
        each_sibling(lambda step: whole_pass(t, step).wait_recv())

    key_count = group * slots * length

    def tile_of(buf):
        def read(index, tile):
            if tile == key_count:
                return buf[...].reshape(key_count, size)
            blocks = tile // length
            per = slots // blocks
            if per == 0:
                rows = blocks // slots
                return buf[pl.ds(index * rows, rows)].reshape(tile, size)
            first = lax.rem(index, per) * blocks
            return buf[lax.div(index, per), pl.ds(first, blocks)].reshape(tile, size)

        return read

    returned = []
    for first in range(0, slots, SLOTS_AT_ONCE):
        here = range(first, min(first + SLOTS_AT_ONCE, slots))
        for slot in here:
            if slot == own:
                own_copies[2].wait()
            else:
                sent[2][slot].wait_recv()
        rows = len(here) * length
        result = attend(
            qb[first : first + len(here)].reshape(rows, size),
            tile_of(kb),
            tile_of(vb),
            key_count,
            factor,
        )
        ob[first : first + len(here)] = result.reshape(len(here), length, size)
        for slot in here:
            if slot == own:
                copy = pltpu.make_async_copy(ob.at[own], o_ref.at[my_head], recv_sem.at[3, own])
            else:
                copy = pltpu.make_async_remote_copy(
                    src_ref=ob.at[slot],
                    dst_ref=o_ref.at[my_head],
                    send_sem=send_sem.at[3, slot],
                    recv_sem=recv_sem.at[3, slot],
                    device_id=peer(slot, -1)[0],
                    device_id_type=MESH,
                )
            copy.start()
            returned.append(copy)

    for t in range(2):
        each_sibling(lambda step: whole_pass(t, step).wait_send())
    for row in sent:
        for copy in row:
            copy.wait_send()
    for slot in range(slots):
        returned[slot].wait()


def shards(height, width, token_queries, token_keys, token_values):
    heads, size = token_queries.shape[0], token_queries.shape[-1]
    group = height * width // heads
    blocks = [x.reshape(heads, -1, size) for x in (token_queries, token_keys, token_values)]
    length = blocks[0].shape[1]
    slots = (height // group) * width
    kind = token_queries.dtype
    count = group * slots * length
    pairs = slots * length * count * heads // slots
    out = pl.pallas_call(
        functools.partial(kernel, height, width, group),
        out_shape=jax.ShapeDtypeStruct(blocks[0].shape, kind),
        in_specs=[pl.BlockSpec(memory_space=pl.ANY)] * 3,
        out_specs=pl.BlockSpec(memory_space=pl.ANY),
        scratch_shapes=[
            pltpu.VMEM((slots, length, size), kind),
            pltpu.VMEM((group, slots, length, size), kind),
            pltpu.VMEM((group, slots, length, size), kind),
            pltpu.VMEM((slots, length, size), kind),
            pltpu.SemaphoreType.DMA((4, slots)),
            pltpu.SemaphoreType.DMA((4, slots)),
            pltpu.SemaphoreType.DMA((2, max(group - 1, 1))),
            pltpu.SemaphoreType.DMA((2, max(group - 1, 1))),
        ],
        compiler_params=pltpu.CompilerParams(
            collective_id=0, has_side_effects=True, vmem_limit_bytes=56 * 2**20
        ),
        cost_estimate=pl.CostEstimate(
            flops=4 * pairs * size, bytes_accessed=8 * heads * length * size, transcendentals=pairs
        ),
        name="attention_exchange",
    )(*blocks)
    return out.reshape(token_queries.shape)


def solution(mesh):
    height, width = mesh.shape["ha"], mesh.shape["wa"]
    placed = P(None, None, "ha", "wa", None)
    return jax.shard_map(
        functools.partial(shards, height, width),
        mesh=mesh,
        in_specs=(placed, placed, placed),
        out_specs=placed,
        check_vma=False,
    )
```

```python
import functools
import math

import jax
import jax.numpy as jnp
from jax import lax
from jax.experimental import pallas as pl
from jax.experimental.pallas import tpu as pltpu
from jax.sharding import PartitionSpec as P

MESH = pl.DeviceIdType.MESH
LOG2E = 1.4426950408889634
KEY_TILE = 2048
SLOTS_AT_ONCE = 4


def slot_order(subgroups, width):
    def rank(offset):
        up, across = offset
        distance = min(across, width - across)
        return (-distance, up == 0, across, up)

    return sorted(((u, w) for u in range(subgroups) for w in range(width)), key=rank)


def attend(queries, keys, values, key_count, factor):
    tile = min(KEY_TILE, key_count)
    scale = factor * LOG2E

    def scores_of(index):
        return lax.dot_general(
            queries, keys(index, tile), (((1,), (1,)), ((), ())), preferred_element_type=jnp.float32
        )

    def mix(weights, index):
        return jnp.dot(
            weights.astype(jnp.bfloat16), values(index, tile), preferred_element_type=jnp.float32
        )

    scores = scores_of(0)
    top = jnp.max(scores, axis=1, keepdims=True)
    weights = jnp.exp2((scores - top) * scale)
    total = jnp.sum(weights, axis=1, keepdims=True)
    mixed = mix(weights, 0)

    def fold(index, state):
        top, total, mixed = state
        scores = scores_of(index)
        new_top = jnp.maximum(top, jnp.max(scores, axis=1, keepdims=True))
        shrink = jnp.exp2((top - new_top) * scale)
        weights = jnp.exp2((scores - new_top) * scale)
        total = total * shrink + jnp.sum(weights, axis=1, keepdims=True)
        return new_top, total, mixed * shrink + mix(weights, index)

    if key_count > tile:
        top, total, mixed = lax.fori_loop(1, key_count // tile, fold, (top, total, mixed))
    return (mixed / total).astype(jnp.bfloat16)


def kernel(
    height, width, group, q_ref, k_ref, v_ref, o_ref, qb, kb, vb, ob,
    send_sem, recv_sem, pass_send, pass_recv,
):
    subgroups = height // group
    order = slot_order(subgroups, width)
    slots = len(order)
    own = slots - 1
    length, size = k_ref.shape[1], k_ref.shape[2]
    factor = size ** (-0.5)
    ha, wa = lax.axis_index("ha"), lax.axis_index("wa")
    member, sub = lax.rem(ha, group), lax.div(ha, group)

    def peer(slot, sign):
        up, across = order[slot]
        to_sub = lax.rem(sub + (up if sign > 0 else subgroups - up), subgroups)
        to_wa = lax.rem(wa + (across if sign > 0 else width - across), width)
        return (to_sub * group + member, to_wa), to_sub * width + to_wa

    def sibling(step):
        return (sub * group + lax.rem(member + step, group), wa)

    def each_sibling(act):
        if group == 2:
            act(1)
        elif group > 2:
            pl.loop(1, group)(act)

    my_head = sub * width + wa

    barrier = pltpu.get_barrier_semaphore()
    for slot in range(own):
        pl.semaphore_signal(barrier, inc=1, device_id=peer(slot, 1)[0], device_id_type=MESH)
    each_sibling(
        lambda step: pl.semaphore_signal(
            barrier, inc=1, device_id=sibling(step), device_id_type=MESH
        )
    )
    own_copies = [
        pltpu.make_async_copy(src.at[my_head], dst, recv_sem.at[t, own])
        for t, (src, dst) in enumerate(
            ((k_ref, kb.at[0, own]), (v_ref, vb.at[0, own]), (q_ref, qb.at[own]))
        )
    ]
    for copy in own_copies:
        copy.start()
    pl.semaphore_wait(barrier, own + group - 1)

    def to_peer(t, slot):
        src, dst = ((k_ref, kb.at[0, slot]), (v_ref, vb.at[0, slot]), (q_ref, qb.at[slot]))[t]
        device, head = peer(slot, 1)
        return pltpu.make_async_remote_copy(
            src_ref=src.at[head],
            dst_ref=dst,
            send_sem=send_sem.at[t, slot],
            recv_sem=recv_sem.at[t, slot],
            device_id=device,
            device_id_type=MESH,
        )

    sent = [[to_peer(t, slot) for slot in range(own)] for t in range(3)]
    for t in range(2):
        for copy in sent[t]:
            copy.start()

    def to_sibling(t, slot, step):
        buf = (kb, vb)[t]
        return pltpu.make_async_remote_copy(
            src_ref=buf.at[0, slot],
            dst_ref=buf.at[step, slot],
            send_sem=pass_send.at[t, step - 1],
            recv_sem=pass_recv.at[t, step - 1],
            device_id=sibling(step),
            device_id_type=MESH,
        )

    for t in range(2):
        for slot in (own, *range(own)):
            if slot == own:
                own_copies[t].wait()
            else:
                sent[t][slot].wait_recv()
            each_sibling(lambda step: to_sibling(t, slot, step).start())
            if t == 1 and slot != own:
                sent[1][slot].wait_send()
                sent[2][slot].start()

    def whole_pass(t, step):
        buf = (kb, vb)[t]
        return pltpu.make_async_remote_copy(
            src_ref=buf.at[0],
            dst_ref=buf.at[step],
            send_sem=pass_send.at[t, step - 1],
            recv_sem=pass_recv.at[t, step - 1],
            device_id=sibling(step),
            device_id_type=MESH,
        )

    for t in range(2):
        each_sibling(lambda step: whole_pass(t, step).wait_recv())

    key_count = group * slots * length

    def tile_of(buf):
        def read(index, tile):
            if tile == key_count:
                return buf[...].reshape(key_count, size)
            blocks = tile // length
            per = slots // blocks
            if per == 0:
                rows = blocks // slots
                return buf[pl.ds(index * rows, rows)].reshape(tile, size)
            first = lax.rem(index, per) * blocks
            return buf[lax.div(index, per), pl.ds(first, blocks)].reshape(tile, size)

        return read

    returned = []
    for first in range(0, slots, SLOTS_AT_ONCE):
        here = range(first, min(first + SLOTS_AT_ONCE, slots))
        for slot in here:
            if slot == own:
                own_copies[2].wait()
            else:
                sent[2][slot].wait_recv()
        rows = len(here) * length
        result = attend(
            qb[first : first + len(here)].reshape(rows, size),
            tile_of(kb),
            tile_of(vb),
            key_count,
            factor,
        )
        ob[first : first + len(here)] = result.reshape(len(here), length, size)
        for slot in here:
            if slot == own:
                copy = pltpu.make_async_copy(ob.at[own], o_ref.at[my_head], recv_sem.at[3, own])
            else:
                copy = pltpu.make_async_remote_copy(
                    src_ref=ob.at[slot],
                    dst_ref=o_ref.at[my_head],
                    send_sem=send_sem.at[3, slot],
                    recv_sem=recv_sem.at[3, slot],
                    device_id=peer(slot, -1)[0],
                    device_id_type=MESH,
                )
            copy.start()
            returned.append(copy)

    for t in range(2):
        each_sibling(lambda step: whole_pass(t, step).wait_send())
    for t in (0, 2):
        for copy in sent[t]:
            copy.wait_send()
    for slot in range(slots):
        returned[slot].wait()


def hand_over(src_ref, dst_ref, sem):
    parts = sem.shape[0]
    rows = src_ref.shape[0] // parts
    copies = [
        pltpu.make_async_copy(
            src_ref.at[pl.ds(i * rows, rows)], dst_ref.at[pl.ds(i * rows, rows)], sem.at[i]
        )
        for i in range(parts)
    ]
    for copy in copies:
        copy.start()
    for copy in copies:
        copy.wait()


def shards(height, width, token_queries, token_keys, token_values):
    heads, size = token_queries.shape[0], token_queries.shape[-1]
    group = height * width // heads
    blocks = [x.reshape(heads, -1, size) for x in (token_queries, token_keys, token_values)]
    length = blocks[0].shape[1]
    slots = (height // group) * width
    kind = token_queries.dtype
    count = group * slots * length
    pairs = slots * length * count * heads // slots
    out = pl.pallas_call(
        functools.partial(kernel, height, width, group),
        out_shape=jax.ShapeDtypeStruct(blocks[0].shape, kind),
        in_specs=[pl.BlockSpec(memory_space=pl.ANY)] * 3,
        out_specs=pl.BlockSpec(memory_space=pl.ANY),
        scratch_shapes=[
            pltpu.VMEM((slots, length, size), kind),
            pltpu.VMEM((group, slots, length, size), kind),
            pltpu.VMEM((group, slots, length, size), kind),
            pltpu.VMEM((slots, length, size), kind),
            pltpu.SemaphoreType.DMA((4, slots)),
            pltpu.SemaphoreType.DMA((4, slots)),
            pltpu.SemaphoreType.DMA((2, max(group - 1, 1))),
            pltpu.SemaphoreType.DMA((2, max(group - 1, 1))),
        ],
        compiler_params=pltpu.CompilerParams(
            collective_id=0, has_side_effects=True, vmem_limit_bytes=56 * 2**20
        ),
        cost_estimate=pl.CostEstimate(
            flops=4 * pairs * size, bytes_accessed=8 * heads * length * size, transcendentals=pairs
        ),
        name="attention_exchange",
    )(*blocks)
    out = pl.pallas_call(
        hand_over,
        out_shape=jax.ShapeDtypeStruct(out.shape, kind),
        in_specs=[pl.BlockSpec(memory_space=pl.ANY)],
        out_specs=pl.BlockSpec(memory_space=pl.ANY),
        scratch_shapes=[pltpu.SemaphoreType.DMA((math.gcd(heads, 4),))],
        cost_estimate=pl.CostEstimate(
            flops=0, bytes_accessed=4 * heads * length * size, transcendentals=0
        ),
        name="hand_over",
    )(out)
    return out.reshape(token_queries.shape)


def solution(mesh):
    height, width = mesh.shape["ha"], mesh.shape["wa"]
    placed = P(None, None, "ha", "wa", None)
    return jax.shard_map(
        functools.partial(shards, height, width),
        mesh=mesh,
        in_specs=(placed, placed, placed),
        out_specs=placed,
        check_vma=False,
    )
```

```python
import functools

import jax
import jax.numpy as jnp
from jax import lax
from jax.experimental import pallas as pl
from jax.experimental.pallas import tpu as pltpu
from jax.sharding import PartitionSpec as P

MESH = pl.DeviceIdType.MESH
LOG2E = 1.4426950408889634
KEY_TILE = 2048
SLOTS_AT_ONCE = 4


def slot_order(subgroups, width):
    def rank(offset):
        up, across = offset
        distance = min(across, width - across)
        return (-distance, up == 0, across, up)

    return sorted(((u, w) for u in range(subgroups) for w in range(width)), key=rank)


def attend(queries, keys, values, key_count, factor):
    tile = min(KEY_TILE, key_count)
    scale = factor * LOG2E

    def scores_of(index):
        return lax.dot_general(
            queries, keys(index, tile), (((1,), (1,)), ((), ())), preferred_element_type=jnp.float32
        )

    def mix(weights, index):
        return jnp.dot(
            weights.astype(jnp.bfloat16), values(index, tile), preferred_element_type=jnp.float32
        )

    scores = scores_of(0)
    top = jnp.max(scores, axis=1, keepdims=True)
    weights = jnp.exp2((scores - top) * scale)
    total = jnp.sum(weights, axis=1, keepdims=True)
    mixed = mix(weights, 0)

    def fold(index, state):
        top, total, mixed = state
        scores = scores_of(index)
        new_top = jnp.maximum(top, jnp.max(scores, axis=1, keepdims=True))
        shrink = jnp.exp2((top - new_top) * scale)
        weights = jnp.exp2((scores - new_top) * scale)
        total = total * shrink + jnp.sum(weights, axis=1, keepdims=True)
        return new_top, total, mixed * shrink + mix(weights, index)

    if key_count > tile:
        top, total, mixed = lax.fori_loop(1, key_count // tile, fold, (top, total, mixed))
    return (mixed / total).astype(jnp.bfloat16)


def kernel(
    height, width, group, q_ref, k_ref, v_ref, o_ref, qb, kb, vb, ob,
    send_sem, recv_sem, pass_send, pass_recv, ready,
):
    subgroups = height // group
    order = slot_order(subgroups, width)
    slots = len(order)
    own = slots - 1
    length, size = k_ref.shape[1], k_ref.shape[2]
    factor = size ** (-0.5)
    ha, wa = lax.axis_index("ha"), lax.axis_index("wa")
    member, sub = lax.rem(ha, group), lax.div(ha, group)

    def peer(slot, sign):
        up, across = order[slot]
        to_sub = lax.rem(sub + (up if sign > 0 else subgroups - up), subgroups)
        to_wa = lax.rem(wa + (across if sign > 0 else width - across), width)
        return (to_sub * group + member, to_wa), to_sub * width + to_wa

    def sibling(step):
        return (sub * group + lax.rem(member + step, group), wa)

    def each_sibling(act):
        if group == 2:
            act(1)
        elif group > 2:
            pl.loop(1, group)(act)

    my_head = sub * width + wa

    barrier = pltpu.get_barrier_semaphore()
    for slot in range(own):
        pl.semaphore_signal(barrier, inc=1, device_id=peer(slot, 1)[0], device_id_type=MESH)

    def tell_later(step):
        @pl.when(member + step < group)
        def _():
            pl.semaphore_signal(barrier, inc=1, device_id=sibling(step), device_id_type=MESH)

    def tell_earlier(step):
        @pl.when(member + step >= group)
        def _():
            pl.semaphore_signal(ready, inc=1, device_id=sibling(step), device_id_type=MESH)

    each_sibling(tell_later)
    own_copies = [
        pltpu.make_async_copy(src.at[my_head], dst, recv_sem.at[t, own])
        for t, (src, dst) in enumerate(
            ((k_ref, kb.at[0, own]), (v_ref, vb.at[0, own]), (q_ref, qb.at[own]))
        )
    ]
    for copy in own_copies:
        copy.start()
    pl.semaphore_wait(barrier, own + member)

    def to_peer(t, slot):
        src, dst = ((k_ref, kb.at[0, slot]), (v_ref, vb.at[0, slot]), (q_ref, qb.at[slot]))[t]
        device, head = peer(slot, 1)
        return pltpu.make_async_remote_copy(
            src_ref=src.at[head],
            dst_ref=dst,
            send_sem=send_sem.at[t, slot],
            recv_sem=recv_sem.at[t, slot],
            device_id=device,
            device_id_type=MESH,
        )

    sent = [[to_peer(t, slot) for slot in range(own)] for t in range(3)]
    for t in range(2):
        for copy in sent[t]:
            copy.start()
    each_sibling(tell_earlier)

    @pl.when(member + 1 < group)
    def _():
        pl.semaphore_wait(ready, group - 1 - member)


    def to_sibling(t, slot, step):
        buf = (kb, vb)[t]
        return pltpu.make_async_remote_copy(
            src_ref=buf.at[0, slot],
            dst_ref=buf.at[step, slot],
            send_sem=pass_send.at[t, step - 1],
            recv_sem=pass_recv.at[t, step - 1],
            device_id=sibling(step),
            device_id_type=MESH,
        )

    for t in range(2):
        for slot in (own, *range(own)):
            if slot == own:
                own_copies[t].wait()
            else:
                sent[t][slot].wait_recv()
            each_sibling(lambda step: to_sibling(t, slot, step).start())
            if t == 1 and slot != own:
                sent[1][slot].wait_send()
                sent[2][slot].start()

    def whole_pass(t, step):
        buf = (kb, vb)[t]
        return pltpu.make_async_remote_copy(
            src_ref=buf.at[0],
            dst_ref=buf.at[step],
            send_sem=pass_send.at[t, step - 1],
            recv_sem=pass_recv.at[t, step - 1],
            device_id=sibling(step),
            device_id_type=MESH,
        )

    for t in range(2):
        each_sibling(lambda step: whole_pass(t, step).wait_recv())

    key_count = group * slots * length

    def tile_of(buf):
        def read(index, tile):
            if tile == key_count:
                return buf[...].reshape(key_count, size)
            blocks = tile // length
            per = slots // blocks
            if per == 0:
                rows = blocks // slots
                return buf[pl.ds(index * rows, rows)].reshape(tile, size)
            first = lax.rem(index, per) * blocks
            return buf[lax.div(index, per), pl.ds(first, blocks)].reshape(tile, size)

        return read

    returned = []
    for first in range(0, slots, SLOTS_AT_ONCE):
        here = range(first, min(first + SLOTS_AT_ONCE, slots))
        for slot in here:
            if slot == own:
                own_copies[2].wait()
            else:
                sent[2][slot].wait_recv()
        rows = len(here) * length
        result = attend(
            qb[first : first + len(here)].reshape(rows, size),
            tile_of(kb),
            tile_of(vb),
            key_count,
            factor,
        )
        ob[first : first + len(here)] = result.reshape(len(here), length, size)
        for slot in here:
            if slot == own:
                copy = pltpu.make_async_copy(ob.at[own], o_ref.at[my_head], recv_sem.at[3, own])
            else:
                copy = pltpu.make_async_remote_copy(
                    src_ref=ob.at[slot],
                    dst_ref=o_ref.at[my_head],
                    send_sem=send_sem.at[3, slot],
                    recv_sem=recv_sem.at[3, slot],
                    device_id=peer(slot, -1)[0],
                    device_id_type=MESH,
                )
            copy.start()
            returned.append(copy)

    for t in range(2):
        each_sibling(lambda step: whole_pass(t, step).wait_send())
    for t in (0, 2):
        for copy in sent[t]:
            copy.wait_send()
    for slot in range(slots):
        returned[slot].wait()


def hand_over(src_ref, dst_ref):
    dst_ref[...] = src_ref[...]


def shards(height, width, token_queries, token_keys, token_values):
    heads, size = token_queries.shape[0], token_queries.shape[-1]
    group = height * width // heads
    blocks = [x.reshape(heads, -1, size) for x in (token_queries, token_keys, token_values)]
    length = blocks[0].shape[1]
    slots = (height // group) * width
    kind = token_queries.dtype
    count = group * slots * length
    pairs = slots * length * count * heads // slots
    out = pl.pallas_call(
        functools.partial(kernel, height, width, group),
        out_shape=jax.ShapeDtypeStruct(blocks[0].shape, kind),
        in_specs=[pl.BlockSpec(memory_space=pl.ANY)] * 3,
        out_specs=pl.BlockSpec(memory_space=pl.ANY),
        scratch_shapes=[
            pltpu.VMEM((slots, length, size), kind),
            pltpu.VMEM((group, slots, length, size), kind),
            pltpu.VMEM((group, slots, length, size), kind),
            pltpu.VMEM((slots, length, size), kind),
            pltpu.SemaphoreType.DMA((4, slots)),
            pltpu.SemaphoreType.DMA((4, slots)),
            pltpu.SemaphoreType.DMA((2, max(group - 1, 1))),
            pltpu.SemaphoreType.DMA((2, max(group - 1, 1))),
            pltpu.SemaphoreType.REGULAR,
        ],
        compiler_params=pltpu.CompilerParams(
            collective_id=0, has_side_effects=True, vmem_limit_bytes=56 * 2**20
        ),
        cost_estimate=pl.CostEstimate(
            flops=4 * pairs * size, bytes_accessed=8 * heads * length * size, transcendentals=pairs
        ),
        name="attention_exchange",
    )(*blocks)
    out = pl.pallas_call(
        hand_over,
        out_shape=jax.ShapeDtypeStruct(out.shape, kind),
        in_specs=[pl.BlockSpec(memory_space=pltpu.VMEM)],
        out_specs=pl.BlockSpec(memory_space=pltpu.VMEM),
        cost_estimate=pl.CostEstimate(
            flops=0, bytes_accessed=4 * heads * length * size, transcendentals=0
        ),
        name="hand_over",
    )(out)
    return out.reshape(token_queries.shape)


def solution(mesh):
    height, width = mesh.shape["ha"], mesh.shape["wa"]
    placed = P(None, None, "ha", "wa", None)
    return jax.shard_map(
        functools.partial(shards, height, width),
        mesh=mesh,
        in_specs=(placed, placed, placed),
        out_specs=placed,
        check_vma=False,
    )
```

```python
import functools

import jax
import jax.numpy as jnp
from jax import lax
from jax.experimental import pallas as pl
from jax.experimental.pallas import tpu as pltpu
from jax.sharding import PartitionSpec as P

MESH = pl.DeviceIdType.MESH
LOG2E = 1.4426950408889634
KEY_TILE = 2048
SLOTS_AT_ONCE = 4


def slot_order(subgroups, width):
    def rank(offset):
        up, across = offset
        distance = min(across, width - across)
        return (-distance, up == 0, across, up)

    return sorted(((u, w) for u in range(subgroups) for w in range(width)), key=rank)


def attend(queries, keys, values, key_count, factor):
    tile = min(KEY_TILE, key_count)
    scale = factor * LOG2E

    def scores_of(index):
        return lax.dot_general(
            queries, keys(index, tile), (((1,), (1,)), ((), ())), preferred_element_type=jnp.float32
        )

    def mix(weights, index):
        return jnp.dot(
            weights.astype(jnp.bfloat16), values(index, tile), preferred_element_type=jnp.float32
        )

    scores = scores_of(0)
    top = jnp.max(scores, axis=1, keepdims=True)
    weights = jnp.exp2((scores - top) * scale)
    total = jnp.sum(weights, axis=1, keepdims=True)
    mixed = mix(weights, 0)

    def fold(index, state):
        top, total, mixed = state
        scores = scores_of(index)
        new_top = jnp.maximum(top, jnp.max(scores, axis=1, keepdims=True))
        shrink = jnp.exp2((top - new_top) * scale)
        weights = jnp.exp2((scores - new_top) * scale)
        total = total * shrink + jnp.sum(weights, axis=1, keepdims=True)
        return new_top, total, mixed * shrink + mix(weights, index)

    if key_count > tile:
        top, total, mixed = lax.fori_loop(1, key_count // tile, fold, (top, total, mixed))
    return (mixed / total).astype(jnp.bfloat16)


def kernel(
    height, width, group, q_ref, k_ref, v_ref, o_ref, qb, kb, vb, ob,
    send_sem, recv_sem, pass_send, pass_recv, ready,
):
    subgroups = height // group
    order = slot_order(subgroups, width)
    slots = len(order)
    own = slots - 1
    length, size = k_ref.shape[1], k_ref.shape[2]
    factor = size ** (-0.5)
    ha, wa = lax.axis_index("ha"), lax.axis_index("wa")
    member, sub = lax.rem(ha, group), lax.div(ha, group)

    def peer(slot, sign):
        up, across = order[slot]
        to_sub = lax.rem(sub + (up if sign > 0 else subgroups - up), subgroups)
        to_wa = lax.rem(wa + (across if sign > 0 else width - across), width)
        return (to_sub * group + member, to_wa), to_sub * width + to_wa

    def sibling(step):
        return (sub * group + lax.rem(member + step, group), wa)

    def each_sibling(act):
        if group == 2:
            act(1)
        elif group > 2:
            pl.loop(1, group)(act)

    my_head = sub * width + wa

    barrier = pltpu.get_barrier_semaphore()
    for slot in range(own):
        pl.semaphore_signal(barrier, inc=1, device_id=peer(slot, 1)[0], device_id_type=MESH)

    def tell_later(step):
        @pl.when(member + step < group)
        def _():
            pl.semaphore_signal(barrier, inc=1, device_id=sibling(step), device_id_type=MESH)

    def tell_earlier(step):
        @pl.when(member + step >= group)
        def _():
            pl.semaphore_signal(ready, inc=1, device_id=sibling(step), device_id_type=MESH)

    each_sibling(tell_later)
    own_copies = [
        pltpu.make_async_copy(src.at[my_head], dst, recv_sem.at[t, own])
        for t, (src, dst) in enumerate(
            ((k_ref, kb.at[0, own]), (v_ref, vb.at[0, own]), (q_ref, qb.at[own]))
        )
    ]
    for copy in own_copies:
        copy.start()
    pl.semaphore_wait(barrier, own + member)

    def to_peer(t, slot):
        src, dst = ((k_ref, kb.at[0, slot]), (v_ref, vb.at[0, slot]), (q_ref, qb.at[slot]))[t]
        device, head = peer(slot, 1)
        return pltpu.make_async_remote_copy(
            src_ref=src.at[head],
            dst_ref=dst,
            send_sem=send_sem.at[t, slot],
            recv_sem=recv_sem.at[t, slot],
            device_id=device,
            device_id_type=MESH,
        )

    sent = [[to_peer(t, slot) for slot in range(own)] for t in range(3)]
    for t in range(2):
        for copy in sent[t]:
            copy.start()

    @pl.when(member == 0)
    def _():
        for copy in sent[2]:
            copy.start()

    each_sibling(tell_earlier)

    @pl.when(member + 1 < group)
    def _():
        pl.semaphore_wait(ready, group - 1 - member)


    def to_sibling(t, slot, step):
        buf = (kb, vb)[t]
        return pltpu.make_async_remote_copy(
            src_ref=buf.at[0, slot],
            dst_ref=buf.at[step, slot],
            send_sem=pass_send.at[t, step - 1],
            recv_sem=pass_recv.at[t, step - 1],
            device_id=sibling(step),
            device_id_type=MESH,
        )

    for t in range(2):
        for slot in (own, *range(own)):
            if slot == own:
                own_copies[t].wait()
            else:
                sent[t][slot].wait_recv()
            each_sibling(lambda step: to_sibling(t, slot, step).start())
            if t == 1 and slot != own:
                sent[1][slot].wait_send()
                pl.when(member > 0)(sent[2][slot].start)

    def whole_pass(t, step):
        buf = (kb, vb)[t]
        return pltpu.make_async_remote_copy(
            src_ref=buf.at[0],
            dst_ref=buf.at[step],
            send_sem=pass_send.at[t, step - 1],
            recv_sem=pass_recv.at[t, step - 1],
            device_id=sibling(step),
            device_id_type=MESH,
        )

    for t in range(2):
        each_sibling(lambda step: whole_pass(t, step).wait_recv())

    key_count = group * slots * length

    def tile_of(buf):
        def read(index, tile):
            if tile == key_count:
                return buf[...].reshape(key_count, size)
            blocks = tile // length
            per = slots // blocks
            if per == 0:
                rows = blocks // slots
                return buf[pl.ds(index * rows, rows)].reshape(tile, size)
            first = lax.rem(index, per) * blocks
            return buf[lax.div(index, per), pl.ds(first, blocks)].reshape(tile, size)

        return read

    returned = []
    for first in range(0, slots, SLOTS_AT_ONCE):
        here = range(first, min(first + SLOTS_AT_ONCE, slots))
        for slot in here:
            if slot == own:
                own_copies[2].wait()
            else:
                sent[2][slot].wait_recv()
        rows = len(here) * length
        result = attend(
            qb[first : first + len(here)].reshape(rows, size),
            tile_of(kb),
            tile_of(vb),
            key_count,
            factor,
        )
        ob[first : first + len(here)] = result.reshape(len(here), length, size)
        for slot in here:
            if slot == own:
                copy = pltpu.make_async_copy(ob.at[own], o_ref.at[my_head], recv_sem.at[3, own])
            else:
                copy = pltpu.make_async_remote_copy(
                    src_ref=ob.at[slot],
                    dst_ref=o_ref.at[my_head],
                    send_sem=send_sem.at[3, slot],
                    recv_sem=recv_sem.at[3, slot],
                    device_id=peer(slot, -1)[0],
                    device_id_type=MESH,
                )
            copy.start()
            returned.append(copy)

    for t in range(2):
        each_sibling(lambda step: whole_pass(t, step).wait_send())
    for t in (0, 2):
        for copy in sent[t]:
            copy.wait_send()
    for slot in range(slots):
        returned[slot].wait()


def hand_over(src_ref, dst_ref):
    dst_ref[...] = src_ref[...]


def shards(height, width, token_queries, token_keys, token_values):
    heads, size = token_queries.shape[0], token_queries.shape[-1]
    group = height * width // heads
    blocks = [x.reshape(heads, -1, size) for x in (token_queries, token_keys, token_values)]
    length = blocks[0].shape[1]
    slots = (height // group) * width
    kind = token_queries.dtype
    count = group * slots * length
    pairs = slots * length * count * heads // slots
    out = pl.pallas_call(
        functools.partial(kernel, height, width, group),
        out_shape=jax.ShapeDtypeStruct(blocks[0].shape, kind),
        in_specs=[pl.BlockSpec(memory_space=pl.ANY)] * 3,
        out_specs=pl.BlockSpec(memory_space=pl.ANY),
        scratch_shapes=[
            pltpu.VMEM((slots, length, size), kind),
            pltpu.VMEM((group, slots, length, size), kind),
            pltpu.VMEM((group, slots, length, size), kind),
            pltpu.VMEM((slots, length, size), kind),
            pltpu.SemaphoreType.DMA((4, slots)),
            pltpu.SemaphoreType.DMA((4, slots)),
            pltpu.SemaphoreType.DMA((2, max(group - 1, 1))),
            pltpu.SemaphoreType.DMA((2, max(group - 1, 1))),
            pltpu.SemaphoreType.REGULAR,
        ],
        compiler_params=pltpu.CompilerParams(
            collective_id=0, has_side_effects=True, vmem_limit_bytes=56 * 2**20
        ),
        cost_estimate=pl.CostEstimate(
            flops=4 * pairs * size, bytes_accessed=8 * heads * length * size, transcendentals=pairs
        ),
        name="attention_exchange",
    )(*blocks)
    out = pl.pallas_call(
        hand_over,
        out_shape=jax.ShapeDtypeStruct(out.shape, kind),
        in_specs=[pl.BlockSpec(memory_space=pltpu.VMEM)],
        out_specs=pl.BlockSpec(memory_space=pltpu.VMEM),
        cost_estimate=pl.CostEstimate(
            flops=0, bytes_accessed=4 * heads * length * size, transcendentals=0
        ),
        name="hand_over",
    )(out)
    return out.reshape(token_queries.shape)


def solution(mesh):
    height, width = mesh.shape["ha"], mesh.shape["wa"]
    placed = P(None, None, "ha", "wa", None)
    return jax.shard_map(
        functools.partial(shards, height, width),
        mesh=mesh,
        in_specs=(placed, placed, placed),
        out_specs=placed,
        check_vma=False,
    )
```

```python
import functools

import jax
import jax.numpy as jnp
from jax import lax
from jax.experimental import pallas as pl
from jax.experimental.pallas import tpu as pltpu
from jax.sharding import PartitionSpec as P

MESH = pl.DeviceIdType.MESH
LOG2E = 1.4426950408889634
KEY_TILE = 2048
SLOTS_AT_ONCE = 4


def slot_order(subgroups, width):
    def rank(offset):
        up, across = offset
        distance = min(across, width - across)
        return (-distance, up == 0, across, up)

    return sorted(((u, w) for u in range(subgroups) for w in range(width)), key=rank)


def attend(queries, keys, values, key_count, factor):
    tile = min(KEY_TILE, key_count)
    scale = factor * LOG2E

    def scores_of(index):
        return lax.dot_general(
            queries, keys(index, tile), (((1,), (1,)), ((), ())), preferred_element_type=jnp.float32
        )

    def mix(weights, index):
        return jnp.dot(
            weights.astype(jnp.bfloat16), values(index, tile), preferred_element_type=jnp.float32
        )

    scores = scores_of(0)
    top = jnp.max(scores, axis=1, keepdims=True)
    weights = jnp.exp2((scores - top) * scale)
    total = jnp.sum(weights, axis=1, keepdims=True)
    mixed = mix(weights, 0)

    def fold(index, state):
        top, total, mixed = state
        scores = scores_of(index)
        new_top = jnp.maximum(top, jnp.max(scores, axis=1, keepdims=True))
        shrink = jnp.exp2((top - new_top) * scale)
        weights = jnp.exp2((scores - new_top) * scale)
        total = total * shrink + jnp.sum(weights, axis=1, keepdims=True)
        return new_top, total, mixed * shrink + mix(weights, index)

    if key_count > tile:
        top, total, mixed = lax.fori_loop(1, key_count // tile, fold, (top, total, mixed))
    return (mixed / total).astype(jnp.bfloat16)


def kernel(
    height, width, group, q_ref, k_ref, v_ref, o_ref, qb, kb, vb, ob,
    send_sem, recv_sem, pass_send, pass_recv, ready, here,
):
    subgroups = height // group
    order = slot_order(subgroups, width)
    slots = len(order)
    own = slots - 1
    length, size = k_ref.shape[1], k_ref.shape[2]
    factor = size ** (-0.5)
    ha, wa = lax.axis_index("ha"), lax.axis_index("wa")
    member, sub = lax.rem(ha, group), lax.div(ha, group)

    def peer(slot, sign):
        up, across = order[slot]
        to_sub = lax.rem(sub + (up if sign > 0 else subgroups - up), subgroups)
        to_wa = lax.rem(wa + (across if sign > 0 else width - across), width)
        return (to_sub * group + member, to_wa), to_sub * width + to_wa

    def sibling(step):
        return (sub * group + lax.rem(member + step, group), wa)

    def each_sibling(act):
        if group == 2:
            act(1)
        elif group > 2:
            pl.loop(1, group)(act)

    my_head = sub * width + wa

    place = wa * subgroups + sub

    def is_before(slot):
        (to_ha, to_wa), _ = peer(slot, 1)
        return to_wa * subgroups + lax.div(to_ha, group) < place

    before = [is_before(slot) for slot in range(own)]
    barrier = pltpu.get_barrier_semaphore()

    def tell_peer(slot, semaphore):
        pl.semaphore_signal(semaphore, inc=1, device_id=peer(slot, 1)[0], device_id_type=MESH)

    for slot in range(own):
        pl.when(~before[slot])(functools.partial(tell_peer, slot, barrier))

    def tell_later(step):
        @pl.when(member + step < group)
        def _():
            pl.semaphore_signal(barrier, inc=1, device_id=sibling(step), device_id_type=MESH)

    def tell_earlier(step):
        @pl.when(member + step >= group)
        def _():
            pl.semaphore_signal(ready, inc=1, device_id=sibling(step), device_id_type=MESH)

    each_sibling(tell_later)
    own_copies = [
        pltpu.make_async_copy(src.at[my_head], dst, recv_sem.at[t, own])
        for t, (src, dst) in enumerate(
            ((k_ref, kb.at[0, own]), (v_ref, vb.at[0, own]), (q_ref, qb.at[own]))
        )
    ]
    for copy in own_copies:
        copy.start()

    @pl.when(place + member > 0)
    def _():
        pl.semaphore_wait(barrier, place + member)

    for slot in range(own):
        up, across = order[slot]
        back = order.index(((subgroups - up) % subgroups, (width - across) % width))
        pl.when(before[slot])(functools.partial(tell_peer, slot, here.at[back]))

    def to_peer(t, slot):
        src, dst = ((k_ref, kb.at[0, slot]), (v_ref, vb.at[0, slot]), (q_ref, qb.at[slot]))[t]
        device, head = peer(slot, 1)
        return pltpu.make_async_remote_copy(
            src_ref=src.at[head],
            dst_ref=dst,
            send_sem=send_sem.at[t, slot],
            recv_sem=recv_sem.at[t, slot],
            device_id=device,
            device_id_type=MESH,
        )

    sent = [[to_peer(t, slot) for slot in range(own)] for t in range(3)]
    for t in range(2):
        for slot in range(own):
            pl.when(before[slot])(sent[t][slot].start)
    for t in range(2):
        for slot in range(own):

            @pl.when(~before[slot])
            def _():
                if t == 0:
                    pl.semaphore_wait(here.at[slot], 1)
                sent[t][slot].start()

    @pl.when(member == 0)
    def _():
        for copy in sent[2]:
            copy.start()

    each_sibling(tell_earlier)

    @pl.when(member + 1 < group)
    def _():
        pl.semaphore_wait(ready, group - 1 - member)


    def to_sibling(t, slot, step):
        buf = (kb, vb)[t]
        return pltpu.make_async_remote_copy(
            src_ref=buf.at[0, slot],
            dst_ref=buf.at[step, slot],
            send_sem=pass_send.at[t, step - 1],
            recv_sem=pass_recv.at[t, step - 1],
            device_id=sibling(step),
            device_id_type=MESH,
        )

    for t in range(2):
        for slot in (own, *range(own)):
            if slot == own:
                own_copies[t].wait()
            else:
                sent[t][slot].wait_recv()
            each_sibling(lambda step: to_sibling(t, slot, step).start())
            if t == 1 and slot != own:
                sent[1][slot].wait_send()
                pl.when(member > 0)(sent[2][slot].start)

    def whole_pass(t, step):
        buf = (kb, vb)[t]
        return pltpu.make_async_remote_copy(
            src_ref=buf.at[0],
            dst_ref=buf.at[step],
            send_sem=pass_send.at[t, step - 1],
            recv_sem=pass_recv.at[t, step - 1],
            device_id=sibling(step),
            device_id_type=MESH,
        )

    for t in range(2):
        each_sibling(lambda step: whole_pass(t, step).wait_recv())

    key_count = group * slots * length

    def tile_of(buf):
        def read(index, tile):
            if tile == key_count:
                return buf[...].reshape(key_count, size)
            blocks = tile // length
            per = slots // blocks
            if per == 0:
                rows = blocks // slots
                return buf[pl.ds(index * rows, rows)].reshape(tile, size)
            first = lax.rem(index, per) * blocks
            return buf[lax.div(index, per), pl.ds(first, blocks)].reshape(tile, size)

        return read

    returned = []
    for first in range(0, slots, SLOTS_AT_ONCE):
        chunk = range(first, min(first + SLOTS_AT_ONCE, slots))
        for slot in chunk:
            if slot == own:
                own_copies[2].wait()
            else:
                sent[2][slot].wait_recv()
        rows = len(chunk) * length
        result = attend(
            qb[first : first + len(chunk)].reshape(rows, size),
            tile_of(kb),
            tile_of(vb),
            key_count,
            factor,
        )
        ob[first : first + len(chunk)] = result.reshape(len(chunk), length, size)
        for slot in chunk:
            if slot == own:
                copy = pltpu.make_async_copy(ob.at[own], o_ref.at[my_head], recv_sem.at[3, own])
            else:
                copy = pltpu.make_async_remote_copy(
                    src_ref=ob.at[slot],
                    dst_ref=o_ref.at[my_head],
                    send_sem=send_sem.at[3, slot],
                    recv_sem=recv_sem.at[3, slot],
                    device_id=peer(slot, -1)[0],
                    device_id_type=MESH,
                )
            copy.start()
            returned.append(copy)

    for t in range(2):
        each_sibling(lambda step: whole_pass(t, step).wait_send())
    for t in (0, 2):
        for copy in sent[t]:
            copy.wait_send()
    for slot in range(slots):
        returned[slot].wait()


def hand_over(src_ref, dst_ref):
    dst_ref[...] = src_ref[...]


def shards(height, width, token_queries, token_keys, token_values):
    heads, size = token_queries.shape[0], token_queries.shape[-1]
    group = height * width // heads
    blocks = [x.reshape(heads, -1, size) for x in (token_queries, token_keys, token_values)]
    length = blocks[0].shape[1]
    slots = (height // group) * width
    kind = token_queries.dtype
    count = group * slots * length
    pairs = slots * length * count * heads // slots
    out = pl.pallas_call(
        functools.partial(kernel, height, width, group),
        out_shape=jax.ShapeDtypeStruct(blocks[0].shape, kind),
        in_specs=[pl.BlockSpec(memory_space=pl.ANY)] * 3,
        out_specs=pl.BlockSpec(memory_space=pl.ANY),
        scratch_shapes=[
            pltpu.VMEM((slots, length, size), kind),
            pltpu.VMEM((group, slots, length, size), kind),
            pltpu.VMEM((group, slots, length, size), kind),
            pltpu.VMEM((slots, length, size), kind),
            pltpu.SemaphoreType.DMA((4, slots)),
            pltpu.SemaphoreType.DMA((4, slots)),
            pltpu.SemaphoreType.DMA((2, max(group - 1, 1))),
            pltpu.SemaphoreType.DMA((2, max(group - 1, 1))),
            pltpu.SemaphoreType.REGULAR,
            pltpu.SemaphoreType.REGULAR((slots,)),
        ],
        compiler_params=pltpu.CompilerParams(
            collective_id=0, has_side_effects=True, vmem_limit_bytes=56 * 2**20
        ),
        cost_estimate=pl.CostEstimate(
            flops=4 * pairs * size, bytes_accessed=8 * heads * length * size, transcendentals=pairs
        ),
        name="attention_exchange",
    )(*blocks)
    out = pl.pallas_call(
        hand_over,
        out_shape=jax.ShapeDtypeStruct(out.shape, kind),
        in_specs=[pl.BlockSpec(memory_space=pltpu.VMEM)],
        out_specs=pl.BlockSpec(memory_space=pltpu.VMEM),
        cost_estimate=pl.CostEstimate(
            flops=0, bytes_accessed=4 * heads * length * size, transcendentals=0
        ),
        name="hand_over",
    )(out)
    return out.reshape(token_queries.shape)


def solution(mesh):
    height, width = mesh.shape["ha"], mesh.shape["wa"]
    placed = P(None, None, "ha", "wa", None)
    return jax.shard_map(
        functools.partial(shards, height, width),
        mesh=mesh,
        in_specs=(placed, placed, placed),
        out_specs=placed,
        check_vma=False,
    )
```

```python
import functools

import jax
import jax.numpy as jnp
from jax import lax
from jax.experimental import pallas as pl
from jax.experimental.pallas import tpu as pltpu
from jax.sharding import PartitionSpec as P

MESH = pl.DeviceIdType.MESH
LOG2E = 1.4426950408889634
KEY_TILE = 2048
SLOTS_AT_ONCE = 4


def swaps(count):
    return count & (count - 1) == 0


def slot_order(subgroups, width):
    def rank(offset):
        up, across = offset
        far = across.bit_length() if swaps(width) else min(across, width - across)
        return (-far, up == 0, up, across)

    return sorted(((u, w) for u in range(subgroups) for w in range(width)), key=rank)


def partner(index, offset, count, sign):
    if not swaps(count):
        return lax.rem(index + (offset if sign > 0 else count - offset), count)
    for bit in range(offset.bit_length()):
        step = 1 << bit
        if offset & step:
            index = index + step - 2 * step * lax.rem(lax.div(index, step), 2)
    return index


def attend(queries, keys, values, key_count, factor):
    tile = min(KEY_TILE, key_count)
    scale = factor * LOG2E

    def scores_of(index):
        return lax.dot_general(
            queries, keys(index, tile), (((1,), (1,)), ((), ())), preferred_element_type=jnp.float32
        )

    def mix(weights, index):
        return jnp.dot(
            weights.astype(jnp.bfloat16), values(index, tile), preferred_element_type=jnp.float32
        )

    scores = scores_of(0)
    top = jnp.max(scores, axis=1, keepdims=True)
    weights = jnp.exp2((scores - top) * scale)
    total = jnp.sum(weights, axis=1, keepdims=True)
    mixed = mix(weights, 0)

    def fold(index, state):
        top, total, mixed = state
        scores = scores_of(index)
        new_top = jnp.maximum(top, jnp.max(scores, axis=1, keepdims=True))
        shrink = jnp.exp2((top - new_top) * scale)
        weights = jnp.exp2((scores - new_top) * scale)
        total = total * shrink + jnp.sum(weights, axis=1, keepdims=True)
        return new_top, total, mixed * shrink + mix(weights, index)

    if key_count > tile:
        top, total, mixed = lax.fori_loop(1, key_count // tile, fold, (top, total, mixed))
    return (mixed / total).astype(jnp.bfloat16)


def kernel(
    height, width, group, q_ref, k_ref, v_ref, o_ref, qb, kb, vb, ob,
    send_sem, recv_sem, pass_send, pass_recv, ready,
):
    subgroups = height // group
    order = slot_order(subgroups, width)
    slots = len(order)
    own = slots - 1
    length, size = k_ref.shape[1], k_ref.shape[2]
    factor = size ** (-0.5)
    ha, wa = lax.axis_index("ha"), lax.axis_index("wa")
    member, sub = lax.rem(ha, group), lax.div(ha, group)

    def peer(slot, sign):
        up, across = order[slot]
        to_sub = partner(sub, up, subgroups, sign)
        to_wa = partner(wa, across, width, sign)
        return (to_sub * group + member, to_wa), to_sub * width + to_wa

    def sibling(step):
        return (sub * group + lax.rem(member + step, group), wa)

    def each_sibling(act):
        if group == 2:
            act(1)
        elif group > 2:
            pl.loop(1, group)(act)

    my_head = sub * width + wa

    barrier = pltpu.get_barrier_semaphore()
    for slot in range(own):
        pl.semaphore_signal(barrier, inc=1, device_id=peer(slot, 1)[0], device_id_type=MESH)

    def tell_later(step):
        @pl.when(member + step < group)
        def _():
            pl.semaphore_signal(barrier, inc=1, device_id=sibling(step), device_id_type=MESH)

    def tell_earlier(step):
        @pl.when(member + step >= group)
        def _():
            pl.semaphore_signal(ready, inc=1, device_id=sibling(step), device_id_type=MESH)

    each_sibling(tell_later)
    own_copies = [
        pltpu.make_async_copy(src.at[my_head], dst, recv_sem.at[t, own])
        for t, (src, dst) in enumerate(
            ((k_ref, kb.at[0, own]), (v_ref, vb.at[0, own]), (q_ref, qb.at[own]))
        )
    ]
    for copy in own_copies:
        copy.start()
    pl.semaphore_wait(barrier, own + member)

    def to_peer(t, slot):
        src, dst = ((k_ref, kb.at[0, slot]), (v_ref, vb.at[0, slot]), (q_ref, qb.at[slot]))[t]
        device, head = peer(slot, 1)
        return pltpu.make_async_remote_copy(
            src_ref=src.at[head],
            dst_ref=dst,
            send_sem=send_sem.at[t, slot],
            recv_sem=recv_sem.at[t, slot],
            device_id=device,
            device_id_type=MESH,
        )

    sent = [[to_peer(t, slot) for slot in range(own)] for t in range(3)]
    for t in range(2):
        for copy in sent[t]:
            copy.start()

    @pl.when(member == 0)
    def _():
        for copy in sent[2]:
            copy.start()

    each_sibling(tell_earlier)

    @pl.when(member + 1 < group)
    def _():
        pl.semaphore_wait(ready, group - 1 - member)


    def to_sibling(t, slot, step):
        buf = (kb, vb)[t]
        return pltpu.make_async_remote_copy(
            src_ref=buf.at[0, slot],
            dst_ref=buf.at[step, slot],
            send_sem=pass_send.at[t, step - 1],
            recv_sem=pass_recv.at[t, step - 1],
            device_id=sibling(step),
            device_id_type=MESH,
        )

    for t in range(2):
        for slot in (own, *range(own)):
            if slot == own:
                own_copies[t].wait()
            else:
                sent[t][slot].wait_recv()
            each_sibling(lambda step: to_sibling(t, slot, step).start())
            if t == 1 and slot != own:
                sent[1][slot].wait_send()
                pl.when(member > 0)(sent[2][slot].start)

    def whole_pass(t, step):
        buf = (kb, vb)[t]
        return pltpu.make_async_remote_copy(
            src_ref=buf.at[0],
            dst_ref=buf.at[step],
            send_sem=pass_send.at[t, step - 1],
            recv_sem=pass_recv.at[t, step - 1],
            device_id=sibling(step),
            device_id_type=MESH,
        )

    for t in range(2):
        each_sibling(lambda step: whole_pass(t, step).wait_recv())

    key_count = group * slots * length

    def tile_of(buf):
        def read(index, tile):
            if tile == key_count:
                return buf[...].reshape(key_count, size)
            blocks = tile // length
            per = slots // blocks
            if per == 0:
                rows = blocks // slots
                return buf[pl.ds(index * rows, rows)].reshape(tile, size)
            first = lax.rem(index, per) * blocks
            return buf[lax.div(index, per), pl.ds(first, blocks)].reshape(tile, size)

        return read

    returned = []
    for first in range(0, slots, SLOTS_AT_ONCE):
        here = range(first, min(first + SLOTS_AT_ONCE, slots))
        for slot in here:
            if slot == own:
                own_copies[2].wait()
            else:
                sent[2][slot].wait_recv()
        rows = len(here) * length
        result = attend(
            qb[first : first + len(here)].reshape(rows, size),
            tile_of(kb),
            tile_of(vb),
            key_count,
            factor,
        )
        ob[first : first + len(here)] = result.reshape(len(here), length, size)
        for slot in here:
            if slot == own:
                copy = pltpu.make_async_copy(ob.at[own], o_ref.at[my_head], recv_sem.at[3, own])
            else:
                copy = pltpu.make_async_remote_copy(
                    src_ref=ob.at[slot],
                    dst_ref=o_ref.at[my_head],
                    send_sem=send_sem.at[3, slot],
                    recv_sem=recv_sem.at[3, slot],
                    device_id=peer(slot, -1)[0],
                    device_id_type=MESH,
                )
            copy.start()
            returned.append(copy)

    for t in range(2):
        each_sibling(lambda step: whole_pass(t, step).wait_send())
    for t in (0, 2):
        for copy in sent[t]:
            copy.wait_send()
    for slot in range(slots):
        returned[slot].wait()


def hand_over(src_ref, dst_ref):
    dst_ref[...] = src_ref[...]


def shards(height, width, token_queries, token_keys, token_values):
    heads, size = token_queries.shape[0], token_queries.shape[-1]
    group = height * width // heads
    blocks = [x.reshape(heads, -1, size) for x in (token_queries, token_keys, token_values)]
    length = blocks[0].shape[1]
    slots = (height // group) * width
    kind = token_queries.dtype
    count = group * slots * length
    pairs = slots * length * count * heads // slots
    out = pl.pallas_call(
        functools.partial(kernel, height, width, group),
        out_shape=jax.ShapeDtypeStruct(blocks[0].shape, kind),
        in_specs=[pl.BlockSpec(memory_space=pl.ANY)] * 3,
        out_specs=pl.BlockSpec(memory_space=pl.ANY),
        scratch_shapes=[
            pltpu.VMEM((slots, length, size), kind),
            pltpu.VMEM((group, slots, length, size), kind),
            pltpu.VMEM((group, slots, length, size), kind),
            pltpu.VMEM((slots, length, size), kind),
            pltpu.SemaphoreType.DMA((4, slots)),
            pltpu.SemaphoreType.DMA((4, slots)),
            pltpu.SemaphoreType.DMA((2, max(group - 1, 1))),
            pltpu.SemaphoreType.DMA((2, max(group - 1, 1))),
            pltpu.SemaphoreType.REGULAR,
        ],
        compiler_params=pltpu.CompilerParams(
            collective_id=0, has_side_effects=True, vmem_limit_bytes=56 * 2**20
        ),
        cost_estimate=pl.CostEstimate(
            flops=4 * pairs * size, bytes_accessed=8 * heads * length * size, transcendentals=pairs
        ),
        name="attention_exchange",
    )(*blocks)
    out = pl.pallas_call(
        hand_over,
        out_shape=jax.ShapeDtypeStruct(out.shape, kind),
        in_specs=[pl.BlockSpec(memory_space=pltpu.VMEM)],
        out_specs=pl.BlockSpec(memory_space=pltpu.VMEM),
        cost_estimate=pl.CostEstimate(
            flops=0, bytes_accessed=4 * heads * length * size, transcendentals=0
        ),
        name="hand_over",
    )(out)
    return out.reshape(token_queries.shape)


def solution(mesh):
    height, width = mesh.shape["ha"], mesh.shape["wa"]
    placed = P(None, None, "ha", "wa", None)
    return jax.shard_map(
        functools.partial(shards, height, width),
        mesh=mesh,
        in_specs=(placed, placed, placed),
        out_specs=placed,
        check_vma=False,
    )
```
